128 devices in a mesh: loop: 32 (over x, z, y_hi), mp: 4 (over y_lo, core).
Axes of the slice: x: 4, y: 4 (y_hi: 2, y_lo: 2; y = y_hi * 2 + y_lo), z: 4, core: 2. Of those that a mesh axis runs over, the one named last changes fastest.
Arguments:
- image_feat: bfloat16 [16384, 6144], P('loop', 'mp'), may hold values from -6 to 6
- image_weight: bfloat16 [1024, 6144], P(None, 'mp'), may hold values from -0.078125 to 0.078125
- text_feat: bfloat16 [16384, 2048], P('loop', 'mp'), may hold values from -6 to 6
- text_weight: bfloat16 [1024, 2048], P(None, 'mp'), may hold values from -0.125 to 0.125
Outputs:
- image_feat_gradient: bfloat16 [16384, 6144], P('loop', 'mp')
- text_feat_gradient: bfloat16 [16384, 2048], P('loop', 'mp')
- image_weight_gradient: float32 [1024, 6144], P('loop', 'mp')
- text_weight_gradient: float32 [1024, 2048], P('loop', 'mp')
The draws below stay inside these ranges and needn't reach their ends.
All inputs are finite; a program needn't handle non-finite values.
Results may differ from the reference program's by a relative error of at most 0.0096.
Values may be sent and summed in bfloat16 or wider, within the bound.
No kernel may reach another device: no remote copies, remote signals or barrier semaphores. Data moves between devices by JAX's collectives and lax.ppermute only.
A program may use at most 128 MiB of HBM per device.

```python
import jax
import jax.numpy as jnp
from jax import lax

DI = 6144
DT = 2048
E = 1024
B_DEV = 512
BATCH = 16384


def block_levels(own_key, extent, split, least, largest):
    level, own = 1.0, jax.random.fold_in(own_key, 6)
    for dim, shards_of in split:
        heights = jnp.exp(jax.random.uniform(jax.random.fold_in(own, dim), (shards_of,), jnp.float32, least / len(split), largest / len(split)))
        level = level * jnp.repeat(heights, extent[dim] // shards_of).reshape([-1 if axis == dim else 1 for axis in range(len(extent))])
    return level


def gaussian(key, shape, scale, bound, split=(), kind=jnp.bfloat16):
    entries = jax.random.normal(key, shape, jnp.float32) * scale
    if len(split) > 0:
        entries = block_levels(key, shape, split, -0.22, 0.18) * entries
    return jnp.clip(entries, min=-bound, max=bound).astype(kind)


def setup_inputs(seed: int = 0) -> dict:
    seeds = jax.random.split(jax.random.key(seed), 5)
    return {
        "image_feat": gaussian(seeds[0], (BATCH, DI), 1.0, 6.0, ((0, 32), (1, 4))),
        "image_weight": gaussian(seeds[1], (E, DI), DI ** -0.5, 0.078125, ((1, 4),)),
        "text_feat": gaussian(seeds[2], (BATCH, DT), 1.0, 6.0, ((0, 32), (1, 4))),
        "text_weight": gaussian(seeds[3], (E, DT), DT ** -0.5, 0.125, ((1, 4),)),
    }


logit_scale = 117.0
logit_bias = -12.7
loss_scale = 32768.0
epsilon = 1e-06

def normalize(raw_rows):
    inverse = lax.rsqrt(lax.optimization_barrier(jnp.sum(raw_rows * raw_rows, axis=1, keepdims=True)) + epsilon)
    return (raw_rows * inverse, inverse)

def back_norm(gradient, unit_rows, inverse):
    inner = lax.optimization_barrier(jnp.sum(unit_rows * gradient, axis=1, keepdims=True))
    return (inverse * (gradient - unit_rows * inner)).astype(jnp.bfloat16)

def reference(image_feat, image_weight, text_feat, text_weight):
    contract = (((1,), (1,)), ((), ()))
    leading = (((0,), (0,)), ((), ()))
    image_raw = lax.dot_general(image_feat, image_weight, contract, preferred_element_type=jnp.float32)
    text_raw = lax.dot_general(text_feat, text_weight, contract, preferred_element_type=jnp.float32)
    image_unit, image_inverse = normalize(image_raw)
    text_unit, text_inverse = normalize(text_raw)
    image_embed = image_unit.astype(jnp.bfloat16)
    text_embed = text_unit.astype(jnp.bfloat16)
    blocks = BATCH // B_DEV
    factor = loss_scale * logit_scale / BATCH
    columns = jnp.arange(BATCH, dtype=jnp.int32)

    def one_block(totals, scanned):
        block_unit, block_index = scanned
        logits = logit_scale * lax.dot_general(block_unit, text_embed, contract, preferred_element_type=jnp.float32) + logit_bias
        image_rows = block_index * B_DEV + jnp.arange(B_DEV, dtype=jnp.int32)
        matched = (image_rows[:, None] == columns[None, :]).astype(jnp.float32)
        coefficient = (factor * (jax.nn.sigmoid(logits) - matched)).astype(jnp.bfloat16)
        grad_rows = jnp.dot(coefficient, text_embed, preferred_element_type=jnp.float32)
        totals = totals + lax.dot_general(coefficient, block_unit, leading, preferred_element_type=jnp.float32)
        return (totals, grad_rows)
    text_embed_gradient, grad_blocks = lax.scan(one_block, jnp.zeros((BATCH, E), jnp.float32), (image_embed.reshape(blocks, B_DEV, E), jnp.arange(blocks, dtype=jnp.int32)))
    image_embed_gradient = grad_blocks.reshape(BATCH, E)
    image_raw_gradient = back_norm(image_embed_gradient, image_unit, image_inverse)
    text_raw_gradient = back_norm(text_embed_gradient, text_unit, text_inverse)
    image_feat_gradient = jnp.dot(image_raw_gradient, image_weight, preferred_element_type=jnp.float32).astype(jnp.bfloat16)
    text_feat_gradient = jnp.dot(text_raw_gradient, text_weight, preferred_element_type=jnp.float32).astype(jnp.bfloat16)
    image_weight_gradient = lax.dot_general(image_raw_gradient, image_feat, leading, preferred_element_type=jnp.float32)
    text_weight_gradient = lax.dot_general(text_raw_gradient, text_feat, leading, preferred_element_type=jnp.float32)
    return (image_feat_gradient, text_feat_gradient, image_weight_gradient, text_weight_gradient)
```

```python
import jax
import jax.numpy as jnp
from jax import lax
from jax.sharding import Mesh, PartitionSpec as P

logit_scale = 117.0
logit_bias = -12.7
loss_scale = 32768.0
epsilon = 1e-06

bf16 = jnp.bfloat16
f32 = jnp.float32
SIZES = {"x": 4, "z": 4, "yh": 2, "yl": 2, "core": 2}
LOOP = ("x", "z", "yh")
MP = ("yl", "core")
CONTRACT = (((1,), (1,)), ((), ()))
LEADING = (((0,), (0,)), ((), ()))


def shift(value, axis, step):
    if axis == "y":
        return lax.ppermute(value, ("yh", "yl"), [(i, (i + step) % 4) for i in range(4)])
    n = SIZES[axis]
    return lax.ppermute(value, axis, [(i, (i + step) % n) for i in range(n)])


def cat(*parts):
    return jnp.concatenate(parts, axis=0)


def total(first, *rest):
    result = first.astype(f32)
    for part in rest:
        result = result + part.astype(f32)
    return result


def normalize(raw_rows):
    inverse = lax.rsqrt(jnp.sum(raw_rows * raw_rows, axis=1, keepdims=True) + epsilon)
    return (raw_rows * inverse, inverse)


def back_norm(gradient, unit_rows, inverse):
    inner = jnp.sum(unit_rows * gradient, axis=1, keepdims=True)
    return (inverse * (gradient - unit_rows * inner)).astype(bf16)


def half(value, index):
    rows = value.shape[0] // 2
    return lax.dynamic_slice_in_dim(value, index * rows, rows, axis=0)


def sum_over_mp(partial, yl, core):
    got = shift(half(partial, 1 - core).astype(bf16), "core", 1)
    rows = half(partial, core) + got.astype(f32)
    got = shift(half(rows, 1 - yl).astype(bf16), "yl", 1)
    return half(rows, yl) + got.astype(f32)


def gather_over_mp(share, yl, core):
    got = shift(share, "yl", 1)
    first = yl == 0
    rows = jnp.concatenate((jnp.where(first, share, got), jnp.where(first, got, share)), axis=1)
    got = shift(rows, "core", 1)
    first = core == 0
    return jnp.concatenate((jnp.where(first, rows, got), jnp.where(first, got, rows)), axis=1)


def ring_gather(block, axis):
    rows = block.shape[0] // 2
    up, down = shift(block, axis, 1), shift(block, axis, -1)
    far = cat(shift(up[:rows], axis, 1), shift(down[rows:], axis, -1))
    return [block, up, down, far]


STEPS = (1, -1, 2)


def gather_xz(block):
    rows = block.shape[0] // 2
    one = cat(*ring_gather(block[:rows], "x"))
    two = cat(*ring_gather(block[rows:], "z"))
    return ring_gather(one, "z") + ring_gather(two, "x")


def return_parts(parts, axis):
    return total(parts[0], *[shift(p, axis, -s) for p, s in zip(parts[1:], STEPS)])


def scatter_xz(parts):
    one = return_parts(parts[:4], "z").astype(bf16)
    two = return_parts(parts[4:], "x").astype(bf16)
    rows = one.shape[0] // 4
    one = return_parts([one[k * rows : (k + 1) * rows] for k in range(4)], "x")
    two = return_parts([two[k * rows : (k + 1) * rows] for k in range(4)], "z")
    return cat(one, two)


def gather_y_core(block):
    column = cat(block, *[shift(block, "y", s) for s in STEPS])
    return cat(column, shift(column, "core", 1))


def scatter_y_core(rows):
    half_rows = rows.shape[0] // 2
    column = total(rows[:half_rows], shift(rows[half_rows:], "core", 1)).astype(bf16)
    share = half_rows // 4
    return return_parts([column[k * share : (k + 1) * share] for k in range(4)], "y")


def per_device(image_feat, image_weight, text_feat, text_weight):
    yl, core = lax.axis_index("yl"), lax.axis_index("core")
    rows_dev = image_feat.shape[0]
    share = rows_dev // 4
    batch_total = rows_dev * 32
    factor = loss_scale * logit_scale / batch_total

    text_part = lax.dot_general(text_feat, text_weight, CONTRACT, preferred_element_type=f32)
    text_raw = sum_over_mp(text_part, yl, core)
    text_unit, text_inverse = normalize(text_raw)
    image_part = lax.dot_general(image_feat, image_weight, CONTRACT, preferred_element_type=f32)
    image_raw = sum_over_mp(image_part, yl, core)
    image_unit, image_inverse = normalize(image_raw)

    texts = cat(*gather_xz(text_unit.astype(bf16)))
    images = gather_y_core(image_unit.astype(bf16))

    logits = logit_scale * lax.dot_general(images, texts, CONTRACT, preferred_element_type=f32) + logit_bias
    i = lax.broadcasted_iota(jnp.int32, logits.shape, 0)
    j = lax.broadcasted_iota(jnp.int32, logits.shape, 1)
    place = jnp.where(i < share // 2, i, i - share // 2 + texts.shape[0] // 2)
    matched = ((i < share) & (j == place)).astype(f32)
    coefficient = (factor * (jax.nn.sigmoid(logits) - matched)).astype(bf16)
    text_grads = lax.dot_general(coefficient, images, LEADING, preferred_element_type=f32).astype(bf16)
    image_grads = jnp.dot(coefficient, texts, preferred_element_type=f32).astype(bf16)

    step = texts.shape[0] // 8
    text_embed_gradient = scatter_xz([text_grads[k * step : (k + 1) * step] for k in range(8)])
    image_embed_gradient = scatter_y_core(image_grads)
    image_share = back_norm(image_embed_gradient, image_unit, image_inverse)
    text_share = back_norm(text_embed_gradient, text_unit, text_inverse)
    both = gather_over_mp(jnp.stack((text_share, image_share)), yl, core)
    text_raw_gradient, image_raw_gradient = both[0], both[1]

    image_weight_part = lax.dot_general(
        image_raw_gradient, image_feat, LEADING, preferred_element_type=f32
    ).astype(bf16)
    text_weight_part = lax.dot_general(
        text_raw_gradient, text_feat, LEADING, preferred_element_type=f32
    ).astype(bf16)
    parts = jnp.concatenate((image_weight_part, text_weight_part), axis=1)
    parts = parts.reshape(32, parts.shape[0] // 32, parts.shape[1])
    parts = lax.all_to_all(parts, LOOP, 0, 0, tiled=True)
    weight_gradient = jnp.sum(parts.astype(f32), axis=0)
    image_feat_gradient = jnp.dot(image_raw_gradient, image_weight, preferred_element_type=f32).astype(bf16)
    text_feat_gradient = jnp.dot(text_raw_gradient, text_weight, preferred_element_type=f32).astype(bf16)
    columns = image_feat.shape[1]
    return (
        image_feat_gradient,
        text_feat_gradient,
        weight_gradient[:, :columns],
        weight_gradient[:, columns:],
    )


def solution(mesh):
    fine = Mesh(mesh.devices.reshape(tuple(SIZES.values())), tuple(SIZES))
    both = P(LOOP, MP)
    return jax.shard_map(
        per_device,
        mesh=fine,
        in_specs=(both, P(None, MP), both, P(None, MP)),
        out_specs=(both, both, both, both),
        check_vma=False,
    )
```

```python
import jax
import jax.numpy as jnp
from jax import lax
from jax.sharding import Mesh, PartitionSpec as P

logit_scale = 117.0
logit_bias = -12.7
loss_scale = 32768.0
epsilon = 1e-06

bf16 = jnp.bfloat16
f16 = jnp.float16
f32 = jnp.float32
SIZES = {"x": 4, "z": 4, "yh": 2, "yl": 2, "core": 2}
LOOP = ("x", "z", "yh")
MP = ("yl", "core")
CONTRACT = (((1,), (1,)), ((), ()))
LEADING = (((0,), (0,)), ((), ()))


def shift(value, axis, step):
    if axis == "y":
        return lax.ppermute(value, ("yh", "yl"), [(i, (i + step) % 4) for i in range(4)])
    n = SIZES[axis]
    return lax.ppermute(value, axis, [(i, (i + step) % n) for i in range(n)])


def cat(*parts):
    return jnp.concatenate(parts, axis=0)


def total(first, *rest):
    result = first.astype(f32)
    for part in rest:
        result = result + part.astype(f32)
    return result


def normalize(raw_rows):
    inverse = lax.rsqrt(jnp.sum(raw_rows * raw_rows, axis=1, keepdims=True) + epsilon)
    return (raw_rows * inverse, inverse)


def back_norm(gradient, unit_rows, inverse):
    inner = jnp.sum(unit_rows * gradient, axis=1, keepdims=True)
    return (inverse * (gradient - unit_rows * inner)).astype(bf16)


def half(value, index):
    rows = value.shape[0] // 2
    return lax.dynamic_slice_in_dim(value, index * rows, rows, axis=0)


def exchange_scaled(rows, axis):
    peak = jnp.max(jnp.abs(rows), axis=1, keepdims=True)
    exponent = jnp.clip(jnp.ceil(jnp.log2(peak)), -126.0, 126.0)
    scaled = (rows * jnp.exp2(-exponent)).astype(f16)
    column = jnp.broadcast_to(exponent.astype(f16), (rows.shape[0], 128))
    got = shift(jnp.concatenate((scaled, column), axis=1), axis, 1)
    width = rows.shape[1]
    return got[:, :width].astype(f32) * jnp.exp2(got[:, width : width + 1].astype(f32))


def project(feat, weight, yl, core):
    away = lax.dot_general(half(feat, 1 - core), weight, CONTRACT, preferred_element_type=f32)
    got = shift(away, "core", 1)
    rows = lax.dot_general(half(feat, core), weight, CONTRACT, preferred_element_type=f32) + got
    return half(rows, yl) + exchange_scaled(half(rows, 1 - yl), "yl")


def gather_over_mp(share, yl, core):
    got = shift(share, "yl", 1)
    first = yl == 0
    rows = cat(jnp.where(first, share, got), jnp.where(first, got, share))
    got = shift(rows, "core", 1)
    first = core == 0
    return cat(jnp.where(first, rows, got), jnp.where(first, got, rows))


STEPS = (1, -1, 2)


def direct_gather(block, axis):
    return cat(block, *[shift(block, axis, s) for s in STEPS])


def ring_gather(block, axis):
    rows = block.shape[0] // 2
    up, down = shift(block, axis, 1), shift(block, axis, -1)
    far = cat(shift(up[:rows], axis, 1), shift(down[rows:], axis, -1))
    return [block, up, down, far]


def return_parts(parts, axis):
    return total(parts[0], *[shift(p, axis, -s) for p, s in zip(parts[1:], STEPS)])


def split(value, count):
    rows = value.shape[0] // count
    return [value[k * rows : (k + 1) * rows] for k in range(count)]


def gather_y_core(block):
    column = direct_gather(block, "y")
    return cat(column, shift(column, "core", 1))


def scatter_y_core(rows):
    here, there = split(rows, 2)
    column = total(here, shift(there, "core", 1)).astype(bf16)
    return return_parts(split(column, 4), "y")


def scatter_blocks(value, axis, index):
    def block(step):
        return lax.dynamic_index_in_dim(value, (index + step) % 4, axis=0, keepdims=False)

    return total(block(0), *[shift(block(s), axis, s) for s in STEPS])


def pair_gradients(images, texts, factor, own):
    logits = logit_scale * lax.dot_general(images, texts, CONTRACT, preferred_element_type=f32) + logit_bias
    matched = 0.0
    if own:
        i = lax.broadcasted_iota(jnp.int32, logits.shape, 0)
        j = lax.broadcasted_iota(jnp.int32, logits.shape, 1)
        hit = False
        for image_row, text_row, count in own:
            inside = (i >= image_row) & (i < image_row + count)
            hit = hit | (inside & (j - text_row == i - image_row))
        matched = hit.astype(f32)
    coefficient = (factor * (jax.nn.sigmoid(logits) - matched)).astype(bf16)
    text_part = lax.dot_general(coefficient, images, LEADING, preferred_element_type=f32).astype(bf16)
    image_part = jnp.dot(coefficient, texts, preferred_element_type=f32)
    return text_part, image_part


def per_device(image_feat, image_weight, text_feat, text_weight):
    yl, core = lax.axis_index("yl"), lax.axis_index("core")
    rows_dev = image_feat.shape[0]
    share = rows_dev // 4
    batch_total = rows_dev * 32
    factor = loss_scale * logit_scale / batch_total

    text_raw = project(text_feat, text_weight, yl, core)
    image_raw = project(image_feat, image_weight, yl, core)
    text_unit, text_inverse = normalize(text_raw)
    image_unit, image_inverse = normalize(image_raw)

    text_halves = split(text_unit.astype(bf16), 2)
    one = ring_gather(direct_gather(text_halves[0], "x"), "z")
    two = ring_gather(direct_gather(text_halves[1], "z"), "x")
    images = gather_y_core(image_unit.astype(bf16))

    step = one[0].shape[0]
    near = pair_gradients(
        images, cat(one[0], two[0]), factor, [(0, 0, share // 2), (share // 2, step, share // 2)]
    )
    next_ = pair_gradients(images, cat(one[1], one[2], two[1], two[2]), factor, None)
    far = pair_gradients(images, cat(one[3], two[3]), factor, None)
    image_grads = (near[1] + next_[1] + far[1]).astype(bf16)

    near, next_, far = split(near[0], 2), split(next_[0], 4), split(far[0], 2)
    one = return_parts([near[0], next_[0], next_[1], far[0]], "z").astype(bf16)
    two = return_parts([near[1], next_[2], next_[3], far[1]], "x").astype(bf16)
    text_embed_gradient = cat(return_parts(split(one, 4), "x"), return_parts(split(two, 4), "z"))
    image_embed_gradient = scatter_y_core(image_grads)
    image_share = back_norm(image_embed_gradient, image_unit, image_inverse)
    image_raw_gradient = gather_over_mp(image_share, yl, core)
    text_share = back_norm(text_embed_gradient, text_unit, text_inverse)
    text_raw_gradient = gather_over_mp(text_share, yl, core)

    depth = image_weight.shape[0]
    x, z, yh = lax.axis_index("x"), lax.axis_index("z"), lax.axis_index("yh")
    cut = (image_feat.shape[1] + text_feat.shape[1]) // 2

    def weight_part(raw_gradient, feat):
        return lax.dot_general(raw_gradient, feat, LEADING, preferred_element_type=f32).astype(bf16)

    one = weight_part(image_raw_gradient, image_feat[:, :cut])
    one = scatter_blocks(one.reshape(4, depth // 4, cut), "x", x).astype(bf16)
    one = scatter_blocks(one.reshape(4, depth // 16, cut), "z", z)
    two = jnp.concatenate(
        (weight_part(image_raw_gradient, image_feat[:, cut:]), weight_part(text_raw_gradient, text_feat)), axis=1
    )
    two = two.reshape(4, 4, depth // 16, cut).swapaxes(0, 1)
    two = scatter_blocks(two, "z", z).astype(bf16)
    two = scatter_blocks(two, "x", x)
    rows = jnp.concatenate((one, two), axis=1)
    weight_gradient = half(rows, yh) + shift(half(rows, 1 - yh).astype(bf16), "yh", 1).astype(f32)
    image_feat_gradient = jnp.dot(image_raw_gradient, image_weight, preferred_element_type=f32).astype(bf16)
    text_feat_gradient = jnp.dot(text_raw_gradient, text_weight, preferred_element_type=f32).astype(bf16)
    columns = image_feat.shape[1]
    return (
        image_feat_gradient,
        text_feat_gradient,
        weight_gradient[:, :columns],
        weight_gradient[:, columns:],
    )


def solution(mesh):
    fine = Mesh(mesh.devices.reshape(tuple(SIZES.values())), tuple(SIZES))
    both = P(LOOP, MP)
    return jax.shard_map(
        per_device,
        mesh=fine,
        in_specs=(both, P(None, MP), both, P(None, MP)),
        out_specs=(both, both, both, both),
        check_vma=False,
    )
```

```python
import jax
import jax.numpy as jnp
from jax import lax
from jax.sharding import Mesh, PartitionSpec as P

logit_scale = 117.0
logit_bias = -12.7
loss_scale = 32768.0
epsilon = 1e-06

bf16 = jnp.bfloat16
f16 = jnp.float16
f32 = jnp.float32
SIZES = {"x": 4, "z": 4, "yh": 2, "yl": 2, "core": 2}
LOOP = ("x", "z", "yh")
MP = ("yl", "core")
CONTRACT = (((1,), (1,)), ((), ()))
LEADING = (((0,), (0,)), ((), ()))


def shift(value, axis, step):
    if axis == "y":
        return lax.ppermute(value, ("yh", "yl"), [(i, (i + step) % 4) for i in range(4)])
    n = SIZES[axis]
    return lax.ppermute(value, axis, [(i, (i + step) % n) for i in range(n)])


def cat(*parts):
    return jnp.concatenate(parts, axis=0)


def total(first, *rest):
    result = first.astype(f32)
    for part in rest:
        result = result + part.astype(f32)
    return result


def normalize(raw_rows):
    inverse = lax.rsqrt(jnp.sum(raw_rows * raw_rows, axis=1, keepdims=True) + epsilon)
    return (raw_rows * inverse, inverse)


def back_norm(gradient, unit_rows, inverse):
    inner = jnp.sum(unit_rows * gradient, axis=1, keepdims=True)
    return (inverse * (gradient - unit_rows * inner)).astype(bf16)


def half(value, index):
    rows = value.shape[0] // 2
    return lax.dynamic_slice_in_dim(value, index * rows, rows, axis=0)


def exchange_scaled(rows, axis):
    peak = jnp.max(jnp.abs(rows), axis=1, keepdims=True)
    exponent = jnp.clip(jnp.ceil(jnp.log2(peak)), -126.0, 126.0)
    scaled = (rows * jnp.exp2(-exponent)).astype(f16)
    column = jnp.broadcast_to(exponent.astype(f16), (rows.shape[0], 128))
    got = shift(jnp.concatenate((scaled, column), axis=1), axis, 1)
    width = rows.shape[1]
    return got[:, :width].astype(f32) * jnp.exp2(got[:, width : width + 1].astype(f32))


def project(feat, weight, yl, core):
    away = lax.dot_general(half(feat, 1 - core), weight, CONTRACT, preferred_element_type=f32)
    got = shift(away, "core", 1)
    rows = lax.dot_general(half(feat, core), weight, CONTRACT, preferred_element_type=f32) + got
    return half(rows, yl) + exchange_scaled(half(rows, 1 - yl), "yl")


def gather_over_mp(share, yl, core):
    got = shift(share, "yl", 1)
    first = yl == 0
    rows = cat(jnp.where(first, share, got), jnp.where(first, got, share))
    got = shift(rows, "core", 1)
    first = core == 0
    return cat(jnp.where(first, rows, got), jnp.where(first, got, rows))


STEPS = (1, -1, 2)


def direct_gather(block, axis):
    return cat(block, *[shift(block, axis, s) for s in STEPS])


def return_parts(parts, axis):
    return total(parts[0], *[shift(p, axis, -s) for p, s in zip(parts[1:], STEPS)])


def split(value, count):
    rows = value.shape[0] // count
    return [value[k * rows : (k + 1) * rows] for k in range(count)]


def scatter_y_core(rows):
    here, there = split(rows, 2)
    column = total(here, shift(there, "core", 1)).astype(bf16)
    return return_parts(split(column, 4), "y")


def scatter_blocks(value, axis, index, dim):
    def block(step):
        return lax.dynamic_slice_in_dim(value, (index + step) % 4, 1, axis=dim)

    return total(block(0), *[shift(block(s), axis, s) for s in STEPS])


def tie(*values):
    return lax.optimization_barrier(values)


def pair_gradients(images, texts, factor, own):
    logits = logit_scale * lax.dot_general(images, texts, CONTRACT, preferred_element_type=f32) + logit_bias
    matched = 0.0
    if own:
        i = lax.broadcasted_iota(jnp.int32, logits.shape, 0)
        j = lax.broadcasted_iota(jnp.int32, logits.shape, 1)
        hit = False
        for image_row, text_row, count in own:
            inside = (i >= image_row) & (i < image_row + count)
            hit = hit | (inside & (j - text_row == i - image_row))
        matched = hit.astype(f32)
    coefficient = (factor * (jax.nn.sigmoid(logits) - matched)).astype(bf16)
    text_part = lax.dot_general(coefficient, images, LEADING, preferred_element_type=f32).astype(bf16)
    image_part = jnp.dot(coefficient, texts, preferred_element_type=f32)
    return text_part, image_part


def per_device(image_feat, image_weight, text_feat, text_weight):
    yl, core = lax.axis_index("yl"), lax.axis_index("core")
    rows_dev = image_feat.shape[0]
    share = rows_dev // 4
    batch_total = rows_dev * 32
    factor = loss_scale * logit_scale / batch_total

    text_raw = project(text_feat, text_weight, yl, core)
    image_raw = project(image_feat, image_weight, yl, core)
    text_unit, text_inverse = normalize(text_raw)
    image_unit, image_inverse = normalize(image_raw)

    text_halves = split(text_unit.astype(bf16), 2)
    one, two = direct_gather(text_halves[0], "x"), direct_gather(text_halves[1], "z")
    column = direct_gather(image_unit.astype(bf16), "y")
    one, two, column = tie(one, two, column)
    images = cat(column, shift(column, "core", 1))
    step = one.shape[0]
    next_ = [shift(one, "z", 1), shift(one, "z", -1), shift(two, "x", 1), shift(two, "x", -1)]
    near = pair_gradients(
        images, cat(one, two), factor, [(0, 0, share // 2), (share // 2, step, share // 2)]
    )
    near, next_ = tie(near, next_)
    parts = [p for part in next_ for p in split(part, 2)]
    far = [shift(parts[0], "z", 1), shift(parts[3], "z", -1), shift(parts[4], "x", 1), shift(parts[7], "x", -1)]
    next_ = pair_gradients(images, cat(*next_), factor, None)
    far, next_ = tie(far, next_)
    far = pair_gradients(images, cat(*far), factor, None)
    image_grads = (near[1] + next_[1] + far[1]).astype(bf16)

    near, next_, far = split(near[0], 2), split(next_[0], 4), split(far[0], 2)
    one = return_parts([near[0], next_[0], next_[1], far[0]], "z").astype(bf16)
    two = return_parts([near[1], next_[2], next_[3], far[1]], "x").astype(bf16)
    image_embed_gradient = scatter_y_core(image_grads)
    one, two, image_embed_gradient = tie(one, two, image_embed_gradient)
    image_share = back_norm(image_embed_gradient, image_unit, image_inverse)
    image_raw_gradient = gather_over_mp(image_share, yl, core)
    text_embed_gradient = cat(return_parts(split(one, 4), "x"), return_parts(split(two, 4), "z"))
    text_embed_gradient, image_raw_gradient = tie(text_embed_gradient, image_raw_gradient)
    text_share = back_norm(text_embed_gradient, text_unit, text_inverse)

    depth = image_weight.shape[0]
    x, z, yh = lax.axis_index("x"), lax.axis_index("z"), lax.axis_index("yh")
    cut = (image_feat.shape[1] + text_feat.shape[1]) // 2

    def weight_part(raw_gradient, feat):
        part = lax.dot_general(raw_gradient, feat, LEADING, preferred_element_type=f32).astype(bf16)
        return part.reshape(4, 4, depth // 16, feat.shape[1])

    one = weight_part(image_raw_gradient, image_feat[:, :cut])
    two = weight_part(image_raw_gradient, image_feat[:, cut:])
    text_share, one, two = tie(text_share, one, two)
    one = scatter_blocks(one, "x", x, 0)
    two = scatter_blocks(two, "z", z, 1)
    text_raw_gradient = gather_over_mp(text_share, yl, core)
    three = scatter_blocks(weight_part(text_raw_gradient, text_feat), "z", z, 1)
    image_feat_gradient = jnp.dot(image_raw_gradient, image_weight, preferred_element_type=f32).astype(bf16)
    text_feat_gradient = jnp.dot(text_raw_gradient, text_weight, preferred_element_type=f32).astype(bf16)
    one, two, three, image_feat_gradient, text_feat_gradient = tie(
        one, two, three, image_feat_gradient, text_feat_gradient
    )
    one = scatter_blocks(one.astype(bf16), "z", z, 1)
    two = scatter_blocks(jnp.concatenate((two, three), axis=3).astype(bf16), "x", x, 0)
    rows = jnp.concatenate((one, two), axis=3).reshape(depth // 16, 2 * cut)
    weight_gradient = half(rows, yh) + shift(half(rows, 1 - yh).astype(bf16), "yh", 1).astype(f32)
    columns = image_feat.shape[1]
    return (
        image_feat_gradient,
        text_feat_gradient,
        weight_gradient[:, :columns],
        weight_gradient[:, columns:],
    )


def solution(mesh):
    fine = Mesh(mesh.devices.reshape(tuple(SIZES.values())), tuple(SIZES))
    both = P(LOOP, MP)
    return jax.shard_map(
        per_device,
        mesh=fine,
        in_specs=(both, P(None, MP), both, P(None, MP)),
        out_specs=(both, both, both, both),
        check_vma=False,
    )
```

```python
import jax
import jax.numpy as jnp
from jax import lax
from jax.sharding import Mesh, PartitionSpec as P

logit_scale = 117.0
logit_bias = -12.7
loss_scale = 32768.0
epsilon = 1e-06

bf16 = jnp.bfloat16
f16 = jnp.float16
f32 = jnp.float32
SIZES = {"x": 4, "z": 4, "yh": 2, "yl": 2, "core": 2}
LOOP = ("x", "z", "yh")
MP = ("yl", "core")
CONTRACT = (((1,), (1,)), ((), ()))
LEADING = (((0,), (0,)), ((), ()))


def shift(value, axis, step):
    if axis == "y":
        return lax.ppermute(value, ("yh", "yl"), [(i, (i + step) % 4) for i in range(4)])
    n = SIZES[axis]
    return lax.ppermute(value, axis, [(i, (i + step) % n) for i in range(n)])


def cat(*parts):
    return jnp.concatenate(parts, axis=0)


def total(first, *rest):
    result = first.astype(f32)
    for part in rest:
        result = result + part.astype(f32)
    return result


def normalize(raw_rows):
    inverse = lax.rsqrt(jnp.sum(raw_rows * raw_rows, axis=1, keepdims=True) + epsilon)
    return (raw_rows * inverse, inverse)


def back_norm(gradient, unit_rows, inverse):
    inner = jnp.sum(unit_rows * gradient, axis=1, keepdims=True)
    return (inverse * (gradient - unit_rows * inner)).astype(bf16)


def half(value, index):
    rows = value.shape[0] // 2
    return lax.dynamic_slice_in_dim(value, index * rows, rows, axis=0)


def exchange_scaled(rows, axis):
    peak = jnp.max(jnp.abs(rows), axis=1, keepdims=True)
    exponent = jnp.clip(jnp.ceil(jnp.log2(peak)), -126.0, 126.0)
    scaled = (rows * jnp.exp2(-exponent)).astype(f16)
    column = jnp.broadcast_to(exponent.astype(f16), (rows.shape[0], 128))
    got = shift(jnp.concatenate((scaled, column), axis=1), axis, 1)
    width = rows.shape[1]
    return got[:, :width].astype(f32) * jnp.exp2(got[:, width : width + 1].astype(f32))


def project(feat, weight, yl, core):
    away = lax.dot_general(half(feat, 1 - core), weight, CONTRACT, preferred_element_type=f32)
    got = shift(away, "core", 1)
    rows = lax.dot_general(half(feat, core), weight, CONTRACT, preferred_element_type=f32) + got
    return half(rows, yl) + exchange_scaled(half(rows, 1 - yl), "yl")


def gather_over_mp(share, yl, core):
    got = shift(share, "yl", 1)
    first = yl == 0
    rows = cat(jnp.where(first, share, got), jnp.where(first, got, share))
    got = shift(rows, "core", 1)
    first = core == 0
    return cat(jnp.where(first, rows, got), jnp.where(first, got, rows))


STEPS = (1, -1, 2)


def exchange(value, axis, far):
    return lax.ppermute(value, axis, [(i, 3 - i if far else i ^ 1) for i in range(4)])


def double_gather(block, axis):
    pair = cat(block, exchange(block, axis, False))
    return cat(pair, exchange(pair, axis, True))


def halve_scatter(rows, axis):
    here, there = split(rows, 2)
    here = total(here, exchange(there, axis, True))
    here, there = split(here, 2)
    return total(here, exchange(there.astype(bf16), axis, False))


def halve_scatter_at(rows, axis, index):
    here = total(half(rows, index // 2), exchange(half(rows, 1 - index // 2).astype(bf16), axis, True))
    return total(half(here, index % 2), exchange(half(here, 1 - index % 2).astype(bf16), axis, False))


def gather_y_core(block, y, core):
    rows = block.shape[0]
    column = jnp.zeros((4 * rows, block.shape[1]), block.dtype)
    parts = [(0, block)] + [(s, shift(block, "y", s)) for s in STEPS]
    for step, part in parts:
        column = lax.dynamic_update_slice_in_dim(column, part, (y - step) % 4 * rows, axis=0)
    other = shift(column, "core", 1)
    first = core == 0
    return cat(jnp.where(first, column, other), jnp.where(first, other, column))


def return_parts(parts, axis):
    return total(parts[0], *[shift(p, axis, -s) for p, s in zip(parts[1:], STEPS)])


def split(value, count):
    rows = value.shape[0] // count
    return [value[k * rows : (k + 1) * rows] for k in range(count)]


def scatter_blocks(value, axis, index, dim):
    def block(step):
        return lax.dynamic_slice_in_dim(value, (index + step) % 4, 1, axis=dim)

    return total(block(0), *[shift(block(s), axis, s) for s in STEPS])


def tie(*values):
    return lax.optimization_barrier(values)


def after(value, *others):
    return lax.optimization_barrier((value, *others))[0]


def pair_gradients(images, texts, factor, own):
    logits = logit_scale * lax.dot_general(images, texts, CONTRACT, preferred_element_type=f32) + logit_bias
    matched = 0.0
    if own:
        i = lax.broadcasted_iota(jnp.int32, logits.shape, 0)
        j = lax.broadcasted_iota(jnp.int32, logits.shape, 1)
        hit = False
        for image_row, text_row, count in own:
            inside = (j >= text_row) & (j < text_row + count)
            hit = hit | (inside & (j - text_row == i - image_row))
        matched = hit.astype(f32)
    coefficient = (factor * (jax.nn.sigmoid(logits) - matched)).astype(bf16)
    text_part = lax.dot_general(coefficient, images, LEADING, preferred_element_type=f32).astype(bf16)
    image_part = jnp.dot(coefficient, texts, preferred_element_type=f32)
    return text_part, image_part


def per_device(image_feat, image_weight, text_feat, text_weight):
    yl, core = lax.axis_index("yl"), lax.axis_index("core")
    rows_dev = image_feat.shape[0]
    share = rows_dev // 4
    batch_total = rows_dev * 32
    factor = loss_scale * logit_scale / batch_total

    y = 2 * lax.axis_index("yh") + yl
    image_raw = project(image_feat, image_weight, yl, core)
    text_raw = project(text_feat, text_weight, yl, core)
    image_unit, image_inverse = normalize(image_raw)
    text_unit, text_inverse = normalize(text_raw)

    images = gather_y_core(image_unit.astype(bf16), y, core)
    text_halves = split(text_unit.astype(bf16), 2)
    one, two = double_gather(text_halves[0], "x"), double_gather(text_halves[1], "z")
    one, two, images = tie(one, two, images)
    step = one.shape[0]
    own = (core * 4 + y) * share
    next_ = [shift(one, "z", 1), shift(one, "z", -1), shift(two, "x", 1), shift(two, "x", -1)]
    near = pair_gradients(
        images, cat(one, two), factor, [(own, 0, share // 2), (own + share // 2, step, share // 2)]
    )
    near, next_, one, two = tie(near, next_, one, two)
    far = [shift(one, "z", 2), shift(two, "x", 2)]
    next_ = pair_gradients(images, cat(*next_), factor, None)
    far, next_ = tie(far, next_)
    back = split(next_[0], 4)
    back = [shift(back[0], "z", -1), shift(back[1], "z", 1), shift(back[2], "x", -1), shift(back[3], "x", 1)]
    far = pair_gradients(images, cat(*far), factor, None)
    image_grads = (near[1] + next_[1] + far[1]).astype(bf16)
    image_embed_gradient = lax.psum_scatter(image_grads, ("core", "yh", "yl"), scatter_dimension=0, tiled=True)
    far = split(after(far[0], image_grads, *back), 2)
    near = split(near[0], 2)
    one = total(near[0], back[0], back[1], shift(far[0], "z", 2)).astype(bf16)
    two = total(near[1], back[2], back[3], shift(far[1], "x", 2)).astype(bf16)
    one, two = tie(one, two)
    text_embed_gradient = cat(halve_scatter(one, "x"), halve_scatter(two, "z"))
    text_share = back_norm(text_embed_gradient, text_unit, text_inverse)
    text_raw_gradient = gather_over_mp(text_share, yl, core)
    image_share = back_norm(image_embed_gradient.astype(f32), image_unit, image_inverse)
    image_raw_gradient = lax.all_gather(image_share, ("core", "yl"), axis=0, tiled=True)

    depth = image_weight.shape[0]
    x, z, yh = lax.axis_index("x"), lax.axis_index("z"), lax.axis_index("yh")
    cut = (image_feat.shape[1] + text_feat.shape[1]) // 2

    def weight_part(raw_gradient, feat):
        part = lax.dot_general(raw_gradient, feat, LEADING, preferred_element_type=f32).astype(bf16)
        return part.reshape(4, 4, depth // 16, feat.shape[1])

    one = weight_part(image_raw_gradient, image_feat[:, :cut])
    two = jnp.concatenate(
        (weight_part(image_raw_gradient, image_feat[:, cut:]), weight_part(text_raw_gradient, text_feat)), axis=3
    )
    one, two = tie(one, two)
    one = scatter_blocks(one, "x", x, 0)
    two = scatter_blocks(two, "z", z, 1)
    image_feat_gradient = jnp.dot(image_raw_gradient, image_weight, preferred_element_type=f32).astype(bf16)
    text_feat_gradient = jnp.dot(text_raw_gradient, text_weight, preferred_element_type=f32).astype(bf16)
    one, two, image_feat_gradient, text_feat_gradient = tie(one, two, image_feat_gradient, text_feat_gradient)
    one = halve_scatter_at(one.reshape(depth // 4, cut), "z", z)
    two = halve_scatter_at(two.reshape(depth // 4, cut), "x", x)
    rows = jnp.concatenate((one, two), axis=1)
    weight_gradient = half(rows, yh) + shift(half(rows, 1 - yh).astype(bf16), "yh", 1).astype(f32)
    columns = image_feat.shape[1]
    return (
        image_feat_gradient,
        text_feat_gradient,
        weight_gradient[:, :columns],
        weight_gradient[:, columns:],
    )


def solution(mesh):
    fine = Mesh(mesh.devices.reshape(tuple(SIZES.values())), tuple(SIZES))
    both = P(LOOP, MP)
    return jax.shard_map(
        per_device,
        mesh=fine,
        in_specs=(both, P(None, MP), both, P(None, MP)),
        out_specs=(both, both, both, both),
        check_vma=False,
    )
```

```python
import jax
import jax.numpy as jnp
from jax import lax
from jax.sharding import Mesh, PartitionSpec as P

logit_scale = 117.0
logit_bias = -12.7
loss_scale = 32768.0
epsilon = 1e-06

bf16 = jnp.bfloat16
f16 = jnp.float16
f32 = jnp.float32
SIZES = {"x": 4, "z": 4, "yh": 2, "yl": 2, "core": 2}
LOOP = ("x", "z", "yh")
MP = ("yl", "core")
CONTRACT = (((1,), (1,)), ((), ()))
LEADING = (((0,), (0,)), ((), ()))


def shift(value, axis, step):
    if axis == "y":
        return lax.ppermute(value, ("yh", "yl"), [(i, (i + step) % 4) for i in range(4)])
    n = SIZES[axis]
    return lax.ppermute(value, axis, [(i, (i + step) % n) for i in range(n)])


def cat(*parts):
    return jnp.concatenate(parts, axis=0)


def total(first, *rest):
    result = first.astype(f32)
    for part in rest:
        result = result + part.astype(f32)
    return result


def normalize(raw_rows):
    inverse = lax.rsqrt(jnp.sum(raw_rows * raw_rows, axis=1, keepdims=True) + epsilon)
    return (raw_rows * inverse, inverse)


def back_norm(gradient, unit_rows, inverse):
    inner = jnp.sum(unit_rows * gradient, axis=1, keepdims=True)
    return (inverse * (gradient - unit_rows * inner)).astype(bf16)


def half(value, index):
    rows = value.shape[0] // 2
    return lax.dynamic_slice_in_dim(value, index * rows, rows, axis=0)


def exchange_scaled(rows, axis):
    peak = jnp.max(jnp.abs(rows), axis=1, keepdims=True)
    exponent = jnp.clip(jnp.ceil(jnp.log2(peak)), -126.0, 126.0)
    scaled = (rows * jnp.exp2(-exponent)).astype(f16)
    column = jnp.broadcast_to(exponent.astype(f16), (rows.shape[0], 128))
    got = shift(jnp.concatenate((scaled, column), axis=1), axis, 1)
    width = rows.shape[1]
    return got[:, :width].astype(f32) * jnp.exp2(got[:, width : width + 1].astype(f32))


def project(feat, weight, yl, core):
    away = lax.dot_general(half(feat, 1 - core), weight, CONTRACT, preferred_element_type=f32)
    got = shift(away, "core", 1)
    rows = lax.dot_general(half(feat, core), weight, CONTRACT, preferred_element_type=f32) + got
    return half(rows, yl) + exchange_scaled(half(rows, 1 - yl), "yl")


def gather_over_mp(share, yl, core):
    got = shift(share, "yl", 1)
    first = yl == 0
    rows = cat(jnp.where(first, share, got), jnp.where(first, got, share))
    got = shift(rows, "core", 1)
    first = core == 0
    return cat(jnp.where(first, rows, got), jnp.where(first, got, rows))


STEPS = (1, -1, 2)


def direct_gather(block, axis):
    return cat(block, *[shift(block, axis, s) for s in STEPS])


def return_parts(parts, axis):
    return total(parts[0], *[shift(p, axis, -s) for p, s in zip(parts[1:], STEPS)])


def split(value, count):
    rows = value.shape[0] // count
    return [value[k * rows : (k + 1) * rows] for k in range(count)]


def scatter_blocks(value, axis, index, dim):
    def block(step):
        return lax.dynamic_slice_in_dim(value, (index + step) % 4, 1, axis=dim)

    return total(block(0), *[shift(block(s), axis, s) for s in STEPS])


def tie(*values):
    return lax.optimization_barrier(values)


def pair_gradients(images, texts, factor, own):
    logits = logit_scale * lax.dot_general(images, texts, CONTRACT, preferred_element_type=f32) + logit_bias
    matched = 0.0
    if own:
        i = lax.broadcasted_iota(jnp.int32, logits.shape, 0)
        j = lax.broadcasted_iota(jnp.int32, logits.shape, 1)
        hit = False
        for image_row, text_row, count in own:
            inside = (j >= text_row) & (j < text_row + count)
            hit = hit | (inside & (j - text_row == i - image_row))
        matched = hit.astype(f32)
    coefficient = (factor * (jax.nn.sigmoid(logits) - matched)).astype(bf16)
    text_part = lax.dot_general(coefficient, images, LEADING, preferred_element_type=f32).astype(bf16)
    image_part = jnp.dot(coefficient, texts, preferred_element_type=f32)
    return text_part, image_part


def per_device(image_feat, image_weight, text_feat, text_weight):
    yl, core = lax.axis_index("yl"), lax.axis_index("core")
    rows_dev = image_feat.shape[0]
    share = rows_dev // 4
    batch_total = rows_dev * 32
    factor = loss_scale * logit_scale / batch_total

    y = 2 * lax.axis_index("yh") + yl
    image_raw = project(image_feat, image_weight, yl, core)
    text_raw = project(text_feat, text_weight, yl, core)
    image_unit, image_inverse = normalize(image_raw)
    text_unit, text_inverse = normalize(text_raw)

    images = lax.all_gather(image_unit.astype(bf16), ("core", "yh", "yl"), axis=0, tiled=True)
    text_halves = split(text_unit.astype(bf16), 2)
    one, two = tie(direct_gather(text_halves[0], "x"), direct_gather(text_halves[1], "z"))
    step = one.shape[0]
    own = (core * 4 + y) * share
    next_ = [shift(one, "z", 1), shift(one, "z", -1), shift(two, "x", 1), shift(two, "x", -1)]
    near = pair_gradients(
        images, cat(one, two), factor, [(own, 0, share // 2), (own + share // 2, step, share // 2)]
    )
    near, next_, one, two = tie(near, next_, one, two)
    far = [shift(one, "z", 2), shift(two, "x", 2)]
    next_ = pair_gradients(images, cat(*next_), factor, None)
    far, next_ = tie(far, next_)
    far = pair_gradients(images, cat(*far), factor, None)
    image_grads = (near[1] + next_[1] + far[1]).astype(bf16)

    column = half(image_grads, core).astype(f32) + shift(half(image_grads, 1 - core), "core", 1).astype(f32)
    column = column.astype(bf16).reshape(4, share, column.shape[1])
    image_embed_gradient = scatter_blocks(column, "y", y, 0)[0]
    image_share = back_norm(image_embed_gradient, image_unit, image_inverse)
    image_raw_gradient = gather_over_mp(image_share, yl, core)

    near, next_, far = split(near[0], 2), split(next_[0], 4), split(far[0], 2)
    one = return_parts([near[0], next_[0], next_[1], far[0]], "z").astype(bf16)
    two = return_parts([near[1], next_[2], next_[3], far[1]], "x").astype(bf16)
    text_embed_gradient = cat(return_parts(split(one, 4), "x"), return_parts(split(two, 4), "z"))
    text_embed_gradient, image_raw_gradient = tie(text_embed_gradient, image_raw_gradient)
    text_share = back_norm(text_embed_gradient, text_unit, text_inverse)
    text_raw_gradient = gather_over_mp(text_share, yl, core)

    depth = image_weight.shape[0]
    x, z, yh = lax.axis_index("x"), lax.axis_index("z"), lax.axis_index("yh")
    cut = (image_feat.shape[1] + text_feat.shape[1]) // 2

    def weight_part(raw_gradient, feat):
        part = lax.dot_general(raw_gradient, feat, LEADING, preferred_element_type=f32).astype(bf16)
        return part.reshape(4, 4, depth // 16, feat.shape[1])

    one = weight_part(image_raw_gradient, image_feat[:, :cut])
    two = jnp.concatenate(
        (weight_part(image_raw_gradient, image_feat[:, cut:]), weight_part(text_raw_gradient, text_feat)), axis=3
    )
    one = scatter_blocks(one, "x", x, 0)
    two = scatter_blocks(two, "z", z, 1)
    image_feat_gradient = jnp.dot(image_raw_gradient, image_weight, preferred_element_type=f32).astype(bf16)
    text_feat_gradient = jnp.dot(text_raw_gradient, text_weight, preferred_element_type=f32).astype(bf16)
    one, two, image_feat_gradient, text_feat_gradient = tie(one, two, image_feat_gradient, text_feat_gradient)
    one = scatter_blocks(one.astype(bf16), "z", z, 1)
    two = scatter_blocks(two.astype(bf16), "x", x, 0)
    rows = jnp.concatenate((one, two), axis=3).reshape(depth // 16, 2 * cut)
    weight_gradient = half(rows, yh) + shift(half(rows, 1 - yh).astype(bf16), "yh", 1).astype(f32)
    columns = image_feat.shape[1]
    return (
        image_feat_gradient,
        text_feat_gradient,
        weight_gradient[:, :columns],
        weight_gradient[:, columns:],
    )


def solution(mesh):
    fine = Mesh(mesh.devices.reshape(tuple(SIZES.values())), tuple(SIZES))
    both = P(LOOP, MP)
    return jax.shard_map(
        per_device,
        mesh=fine,
        in_specs=(both, P(None, MP), both, P(None, MP)),
        out_specs=(both, both, both, both),
        check_vma=False,
    )
```

```python
import jax
import jax.numpy as jnp
from jax import lax
from jax.sharding import Mesh, PartitionSpec as P

logit_scale = 117.0
logit_bias = -12.7
loss_scale = 32768.0
epsilon = 1e-06

bf16 = jnp.bfloat16
f16 = jnp.float16
f32 = jnp.float32
SIZES = {"x": 4, "z": 4, "yh": 2, "yl": 2, "core": 2}
LOOP = ("x", "z", "yh")
MP = ("yl", "core")
CONTRACT = (((1,), (1,)), ((), ()))
LEADING = (((0,), (0,)), ((), ()))


def shift(value, axis, step):
    if axis == "y":
        return lax.ppermute(value, ("yh", "yl"), [(i, (i + step) % 4) for i in range(4)])
    n = SIZES[axis]
    return lax.ppermute(value, axis, [(i, (i + step) % n) for i in range(n)])


def cat(*parts):
    return jnp.concatenate(parts, axis=0)


def total(first, *rest):
    result = first.astype(f32)
    for part in rest:
        result = result + part.astype(f32)
    return result


def normalize(raw_rows):
    inverse = lax.rsqrt(jnp.sum(raw_rows * raw_rows, axis=1, keepdims=True) + epsilon)
    return (raw_rows * inverse, inverse)


def back_norm(gradient, unit_rows, inverse):
    inner = jnp.sum(unit_rows * gradient, axis=1, keepdims=True)
    return (inverse * (gradient - unit_rows * inner)).astype(bf16)


def half(value, index):
    rows = value.shape[0] // 2
    return lax.dynamic_slice_in_dim(value, index * rows, rows, axis=0)


def exchange_scaled(rows, axis):
    peak = jnp.max(jnp.abs(rows), axis=1, keepdims=True)
    exponent = jnp.clip(jnp.ceil(jnp.log2(peak)), -126.0, 126.0)
    scaled = (rows * jnp.exp2(-exponent)).astype(f16)
    column = jnp.broadcast_to(exponent.astype(f16), (rows.shape[0], 128))
    got = shift(jnp.concatenate((scaled, column), axis=1), axis, 1)
    width = rows.shape[1]
    return got[:, :width].astype(f32) * jnp.exp2(got[:, width : width + 1].astype(f32))


def project(feat, weight, yl, core):
    away = lax.dot_general(half(feat, 1 - core), weight, CONTRACT, preferred_element_type=f32)
    got = shift(away, "core", 1)
    rows = lax.dot_general(half(feat, core), weight, CONTRACT, preferred_element_type=f32) + got
    return half(rows, yl) + exchange_scaled(half(rows, 1 - yl), "yl")


def gather_over_mp(share, yl, core):
    got = shift(share, "yl", 1)
    first = yl == 0
    rows = cat(jnp.where(first, share, got), jnp.where(first, got, share))
    got = shift(rows, "core", 1)
    first = core == 0
    return cat(jnp.where(first, rows, got), jnp.where(first, got, rows))


STEPS = (1, -1, 2)


def direct_gather(block, axis):
    return cat(block, *[shift(block, axis, s) for s in STEPS])


def gather_y_core(block):
    column = direct_gather(block, "y")
    return cat(column, shift(column, "core", 1))


def scatter_y_core(rows):
    here, there = split(rows, 2)
    column = total(here, shift(there, "core", 1)).astype(bf16)
    return return_parts(split(column, 4), "y")


def return_parts(parts, axis):
    return total(parts[0], *[shift(p, axis, -s) for p, s in zip(parts[1:], STEPS)])


def split(value, count):
    rows = value.shape[0] // count
    return [value[k * rows : (k + 1) * rows] for k in range(count)]


def scatter_blocks(value, axis, index, dim):
    def block(step):
        return lax.dynamic_slice_in_dim(value, (index + step) % 4, 1, axis=dim)

    return total(block(0), *[shift(block(s), axis, s) for s in STEPS])


def tie(*values):
    return lax.optimization_barrier(values)


def pair_gradients(images, texts, factor, own):
    logits = logit_scale * lax.dot_general(images, texts, CONTRACT, preferred_element_type=f32) + logit_bias
    matched = 0.0
    if own:
        i = lax.broadcasted_iota(jnp.int32, logits.shape, 0)
        j = lax.broadcasted_iota(jnp.int32, logits.shape, 1)
        hit = False
        for image_row, text_row, count in own:
            inside = (j >= text_row) & (j < text_row + count)
            hit = hit | (inside & (j - text_row == i - image_row))
        matched = hit.astype(f32)
    coefficient = (factor * (jax.nn.sigmoid(logits) - matched)).astype(bf16)
    text_part = lax.dot_general(coefficient, images, LEADING, preferred_element_type=f32).astype(bf16)
    image_part = jnp.dot(coefficient, texts, preferred_element_type=f32)
    return text_part, image_part


def per_device(image_feat, image_weight, text_feat, text_weight):
    yl, core = lax.axis_index("yl"), lax.axis_index("core")
    rows_dev = image_feat.shape[0]
    share = rows_dev // 4
    batch_total = rows_dev * 32
    factor = loss_scale * logit_scale / batch_total

    text_raw = project(text_feat, text_weight, yl, core)
    image_raw = project(image_feat, image_weight, yl, core)
    text_unit, text_inverse = normalize(text_raw)
    image_unit, image_inverse = normalize(image_raw)

    text_halves = split(text_unit.astype(bf16), 2)
    one, two = tie(direct_gather(text_halves[0], "x"), direct_gather(text_halves[1], "z"))
    images = gather_y_core(image_unit.astype(bf16))
    step = one.shape[0]
    next_ = [shift(one, "z", 1), shift(one, "z", -1), shift(two, "x", 1), shift(two, "x", -1)]
    far = [shift(one, "z", 2), shift(two, "x", 2)]
    near = pair_gradients(
        images, cat(one, two), factor, [(0, 0, share // 2), (share // 2, step, share // 2)]
    )
    near, next_, far = tie(near, next_, far)
    far = pair_gradients(images, cat(*far), factor, None)
    next_ = pair_gradients(images, cat(*next_), factor, None)
    image_grads = (near[1] + next_[1] + far[1]).astype(bf16)
    image_share = back_norm(scatter_y_core(image_grads), image_unit, image_inverse)
    image_raw_gradient = gather_over_mp(image_share, yl, core)

    near, next_, far = split(near[0], 2), split(next_[0], 4), split(far[0], 2)
    one = return_parts([near[0], next_[0], next_[1], far[0]], "z").astype(bf16)
    two = return_parts([near[1], next_[2], next_[3], far[1]], "x").astype(bf16)
    text_embed_gradient = cat(return_parts(split(one, 4), "x"), return_parts(split(two, 4), "z"))
    text_embed_gradient, image_raw_gradient = tie(text_embed_gradient, image_raw_gradient)
    text_share = back_norm(text_embed_gradient, text_unit, text_inverse)
    text_raw_gradient = gather_over_mp(text_share, yl, core)

    depth = image_weight.shape[0]
    x, z, yh = lax.axis_index("x"), lax.axis_index("z"), lax.axis_index("yh")
    cut = (image_feat.shape[1] + text_feat.shape[1]) // 2

    def weight_part(raw_gradient, feat):
        part = lax.dot_general(raw_gradient, feat, LEADING, preferred_element_type=f32).astype(bf16)
        return part.reshape(4, 4, depth // 16, feat.shape[1])

    one = weight_part(image_raw_gradient, image_feat[:, :cut])
    two = jnp.concatenate(
        (weight_part(image_raw_gradient, image_feat[:, cut:]), weight_part(text_raw_gradient, text_feat)), axis=3
    )
    one = scatter_blocks(one, "x", x, 0)
    two = scatter_blocks(two, "z", z, 1)
    image_feat_gradient = jnp.dot(image_raw_gradient, image_weight, preferred_element_type=f32).astype(bf16)
    text_feat_gradient = jnp.dot(text_raw_gradient, text_weight, preferred_element_type=f32).astype(bf16)
    one, two, image_feat_gradient, text_feat_gradient = tie(one, two, image_feat_gradient, text_feat_gradient)
    one = scatter_blocks(one.astype(bf16), "z", z, 1)
    two = scatter_blocks(two.astype(bf16), "x", x, 0)
    rows = jnp.concatenate((one, two), axis=3).reshape(depth // 16, 2 * cut)
    weight_gradient = half(rows, yh) + shift(half(rows, 1 - yh).astype(bf16), "yh", 1).astype(f32)
    columns = image_feat.shape[1]
    return (
        image_feat_gradient,
        text_feat_gradient,
        weight_gradient[:, :columns],
        weight_gradient[:, columns:],
    )


def solution(mesh):
    fine = Mesh(mesh.devices.reshape(tuple(SIZES.values())), tuple(SIZES))
    both = P(LOOP, MP)
    return jax.shard_map(
        per_device,
        mesh=fine,
        in_specs=(both, P(None, MP), both, P(None, MP)),
        out_specs=(both, both, both, both),
        check_vma=False,
    )
```

```python
import jax
import jax.numpy as jnp
from jax import lax
from jax.sharding import Mesh, PartitionSpec as P

logit_scale = 117.0
logit_bias = -12.7
loss_scale = 32768.0
epsilon = 1e-06

bf16 = jnp.bfloat16
f16 = jnp.float16
f32 = jnp.float32
SIZES = {"x": 4, "z": 4, "yh": 2, "yl": 2, "core": 2}
LOOP = ("x", "z", "yh")
MP = ("yl", "core")
CONTRACT = (((1,), (1,)), ((), ()))
LEADING = (((0,), (0,)), ((), ()))


def shift(value, axis, step):
    if axis == "y":
        return lax.ppermute(value, ("yh", "yl"), [(i, (i + step) % 4) for i in range(4)])
    n = SIZES[axis]
    return lax.ppermute(value, axis, [(i, (i + step) % n) for i in range(n)])


def cat(*parts):
    return jnp.concatenate(parts, axis=0)


def total(first, *rest):
    result = first.astype(f32)
    for part in rest:
        result = result + part.astype(f32)
    return result


def normalize(raw_rows):
    inverse = lax.rsqrt(jnp.sum(raw_rows * raw_rows, axis=1, keepdims=True) + epsilon)
    return (raw_rows * inverse, inverse)


def back_norm(gradient, unit_rows, inverse):
    inner = jnp.sum(unit_rows * gradient, axis=1, keepdims=True)
    return (inverse * (gradient - unit_rows * inner)).astype(bf16)


def half(value, index):
    rows = value.shape[0] // 2
    return lax.dynamic_slice_in_dim(value, index * rows, rows, axis=0)


def exchange_scaled(rows, axis):
    peak = jnp.max(jnp.abs(rows), axis=1, keepdims=True)
    exponent = jnp.clip(jnp.ceil(jnp.log2(peak)), -126.0, 126.0)
    scaled = (rows * jnp.exp2(-exponent)).astype(f16)
    column = jnp.broadcast_to(exponent.astype(f16), (rows.shape[0], 128))
    got = shift(jnp.concatenate((scaled, column), axis=1), axis, 1)
    width = rows.shape[1]
    return got[:, :width].astype(f32) * jnp.exp2(got[:, width : width + 1].astype(f32))


def project(feat, weight, yl, core):
    away = lax.dot_general(half(feat, 1 - core), weight, CONTRACT, preferred_element_type=f32)
    got = shift(away, "core", 1)
    rows = lax.dot_general(half(feat, core), weight, CONTRACT, preferred_element_type=f32) + got
    return half(rows, yl) + exchange_scaled(half(rows, 1 - yl), "yl")


def gather_over_mp(share, yl, core):
    got = shift(share, "yl", 1)
    first = yl == 0
    rows = cat(jnp.where(first, share, got), jnp.where(first, got, share))
    got = shift(rows, "core", 1)
    first = core == 0
    return cat(jnp.where(first, rows, got), jnp.where(first, got, rows))


STEPS = (1, -1, 2)


def direct_gather(block, axis):
    return cat(block, *[shift(block, axis, s) for s in STEPS])


def return_parts(parts, axis):
    return total(parts[0], *[shift(p, axis, -s) for p, s in zip(parts[1:], STEPS)])


def split(value, count):
    rows = value.shape[0] // count
    return [value[k * rows : (k + 1) * rows] for k in range(count)]


def scatter_blocks(value, axis, index, dim, others=()):
    def block(step):
        return lax.dynamic_slice_in_dim(value, (index + step) % 4, 1, axis=dim)

    return total(after(block(0), *others), *[shift(block(s), axis, s) for s in STEPS])


def tie(*values):
    return lax.optimization_barrier(values)


def after(value, *others):
    return lax.optimization_barrier((value, *others))[0]


def pair_gradients(images, texts, factor, own):
    logits = logit_scale * lax.dot_general(images, texts, CONTRACT, preferred_element_type=f32) + logit_bias
    matched = 0.0
    if own:
        i = lax.broadcasted_iota(jnp.int32, logits.shape, 0)
        j = lax.broadcasted_iota(jnp.int32, logits.shape, 1)
        hit = False
        for image_row, text_row, count in own:
            inside = (j >= text_row) & (j < text_row + count)
            hit = hit | (inside & (j - text_row == i - image_row))
        matched = hit.astype(f32)
    coefficient = (factor * (jax.nn.sigmoid(logits) - matched)).astype(bf16)
    text_part = lax.dot_general(coefficient, images, LEADING, preferred_element_type=f32).astype(bf16)
    image_part = jnp.dot(coefficient, texts, preferred_element_type=f32)
    return text_part, image_part


def per_device(image_feat, image_weight, text_feat, text_weight):
    yl, core = lax.axis_index("yl"), lax.axis_index("core")
    rows_dev = image_feat.shape[0]
    share = rows_dev // 4
    batch_total = rows_dev * 32
    factor = loss_scale * logit_scale / batch_total

    text_raw = project(text_feat, text_weight, yl, core)
    image_raw = project(image_feat, image_weight, yl, core)
    text_unit, text_inverse = normalize(text_raw)
    image_unit, image_inverse = normalize(image_raw)

    text_halves = split(text_unit.astype(bf16), 2)
    one, two = direct_gather(text_halves[0], "x"), direct_gather(text_halves[1], "z")
    column = direct_gather(image_unit.astype(bf16), "y")
    one, two, column = tie(one, two, column)
    images = cat(column, shift(column, "core", 1))
    step = one.shape[0]
    next_ = [shift(one, "z", 1), shift(one, "z", -1), shift(two, "x", 1), shift(two, "x", -1)]
    near = pair_gradients(
        images, cat(one, two), factor, [(0, 0, share // 2), (share // 2, step, share // 2)]
    )
    near, next_ = tie(near, next_)
    parts = [p for part in next_ for p in split(part, 2)]
    far = [shift(parts[0], "z", 1), shift(parts[3], "z", -1), shift(parts[4], "x", 1), shift(parts[7], "x", -1)]
    next_ = pair_gradients(images, cat(*next_), factor, None)
    far, next_ = tie(far, next_)
    back = split(next_[0], 4)
    back = [shift(back[0], "z", -1), shift(back[1], "z", 1), shift(back[2], "x", -1), shift(back[3], "x", 1)]
    far = pair_gradients(images, cat(*far), factor, None)
    image_grads = (near[1] + next_[1] + far[1]).astype(bf16)

    here, there = split(image_grads, 2)
    column = total(here, shift(there, "core", 1)).astype(bf16)
    far = split(after(far[0], column, *back), 2)
    near = split(near[0], 2)
    one = total(near[0], back[0], back[1], shift(far[0], "z", 2)).astype(bf16)
    two = total(near[1], back[2], back[3], shift(far[1], "x", 2)).astype(bf16)
    image_embed_gradient = return_parts(split(column, 4), "y")
    one, two, image_embed_gradient = tie(one, two, image_embed_gradient)
    image_share = back_norm(image_embed_gradient, image_unit, image_inverse)
    image_raw_gradient = gather_over_mp(image_share, yl, core)
    text_embed_gradient = cat(return_parts(split(one, 4), "x"), return_parts(split(two, 4), "z"))
    text_embed_gradient, image_raw_gradient = tie(text_embed_gradient, image_raw_gradient)
    text_share = back_norm(text_embed_gradient, text_unit, text_inverse)
    text_raw_gradient = gather_over_mp(text_share, yl, core)

    depth = image_weight.shape[0]
    x, z, yh = lax.axis_index("x"), lax.axis_index("z"), lax.axis_index("yh")
    cut = image_feat.shape[1] // 6 * 5
    columns = image_feat.shape[1]

    def weight_part(raw_gradient, feat):
        part = lax.dot_general(raw_gradient, feat, LEADING, preferred_element_type=f32).astype(bf16)
        return part.reshape(4, 4, depth // 16, feat.shape[1])

    one = weight_part(image_raw_gradient, image_feat[:, :cut])
    two = jnp.concatenate(
        (weight_part(image_raw_gradient, image_feat[:, cut:]), weight_part(text_raw_gradient, text_feat)), axis=3
    )
    one = scatter_blocks(one, "x", x, 0, [two])
    two = scatter_blocks(two, "z", z, 1)
    image_feat_gradient = jnp.dot(image_raw_gradient, image_weight, preferred_element_type=f32).astype(bf16)
    text_feat_gradient = jnp.dot(text_raw_gradient, text_weight, preferred_element_type=f32).astype(bf16)
    one = scatter_blocks(one.astype(bf16), "z", z, 1)
    two = scatter_blocks(two.astype(bf16), "x", x, 0)
    rows = jnp.concatenate((one, two), axis=3).reshape(depth // 16, columns + text_feat.shape[1])
    got = shift(half(rows, 1 - yh).astype(bf16), "yh", 1)
    rows = half(rows, yh)
    return (
        image_feat_gradient,
        text_feat_gradient,
        total(rows[:, :columns], got[:, :columns]),
        total(rows[:, columns:], got[:, columns:]),
    )


def solution(mesh):
    fine = Mesh(mesh.devices.reshape(tuple(SIZES.values())), tuple(SIZES))
    both = P(LOOP, MP)
    return jax.shard_map(
        per_device,
        mesh=fine,
        in_specs=(both, P(None, MP), both, P(None, MP)),
        out_specs=(both, both, both, both),
        check_vma=False,
    )
```

```python
import jax
import jax.numpy as jnp
from jax import lax
from jax.sharding import Mesh, PartitionSpec as P

logit_scale = 117.0
logit_bias = -12.7
loss_scale = 32768.0
epsilon = 1e-06

bf16 = jnp.bfloat16
f16 = jnp.float16
f32 = jnp.float32
SIZES = {"x": 4, "z": 4, "yh": 2, "yl": 2, "core": 2}
LOOP = ("x", "z", "yh")
MP = ("yl", "core")
CONTRACT = (((1,), (1,)), ((), ()))
LEADING = (((0,), (0,)), ((), ()))


def shift(value, axis, step):
    if axis == "y":
        return lax.ppermute(value, ("yh", "yl"), [(i, (i + step) % 4) for i in range(4)])
    n = SIZES[axis]
    return lax.ppermute(value, axis, [(i, (i + step) % n) for i in range(n)])


def cat(*parts):
    return jnp.concatenate(parts, axis=0)


def total(first, *rest):
    result = first.astype(f32)
    for part in rest:
        result = result + part.astype(f32)
    return result


def normalize(raw_rows):
    inverse = lax.rsqrt(jnp.sum(raw_rows * raw_rows, axis=1, keepdims=True) + epsilon)
    return (raw_rows * inverse, inverse)


def back_norm(gradient, unit_rows, inverse):
    inner = jnp.sum(unit_rows * gradient, axis=1, keepdims=True)
    return (inverse * (gradient - unit_rows * inner)).astype(bf16)


def half(value, index):
    rows = value.shape[0] // 2
    return lax.dynamic_slice_in_dim(value, index * rows, rows, axis=0)


def exchange_scaled(rows, axis):
    peak = jnp.max(jnp.abs(rows), axis=1, keepdims=True)
    exponent = jnp.clip(jnp.ceil(jnp.log2(peak)), -126.0, 126.0)
    scaled = (rows * jnp.exp2(-exponent)).astype(f16)
    column = jnp.broadcast_to(exponent.astype(f16), (rows.shape[0], 128))
    got = shift(jnp.concatenate((scaled, column), axis=1), axis, 1)
    width = rows.shape[1]
    return got[:, :width].astype(f32) * jnp.exp2(got[:, width : width + 1].astype(f32))


def project(feat, weight, core):
    away = lax.dot_general(half(feat, 1 - core), weight, CONTRACT, preferred_element_type=f32)
    return shift(away, "core", 1), lambda: lax.dot_general(
        half(feat, core), weight, CONTRACT, preferred_element_type=f32
    )


def sum_over_yl(rows, yl):
    return half(rows, yl) + exchange_scaled(half(rows, 1 - yl), "yl")


def gather_over_mp(share, yl, core):
    got = shift(share, "yl", 1)
    first = yl == 0
    rows = cat(jnp.where(first, share, got), jnp.where(first, got, share))
    got = shift(rows, "core", 1)
    first = core == 0
    return cat(jnp.where(first, rows, got), jnp.where(first, got, rows))


STEPS = (1, -1, 2)


def direct_gather(block, axis):
    return cat(block, *[shift(block, axis, s) for s in STEPS])


def return_parts(parts, axis):
    return total(parts[0], *[shift(p, axis, -s) for p, s in zip(parts[1:], STEPS)])


def split(value, count):
    rows = value.shape[0] // count
    return [value[k * rows : (k + 1) * rows] for k in range(count)]


def tie(*values):
    return lax.optimization_barrier(values)


def weight_terms(raw_gradient, feat):
    terms = lax.dot_general(raw_gradient, feat, LEADING, preferred_element_type=f32).astype(bf16)
    return terms.reshape(32, terms.shape[0] // 32, terms.shape[1])


def sum_over_loop(terms):
    return jnp.sum(lax.all_to_all(terms, LOOP, 0, 0, tiled=True).astype(f32), axis=0)


def pair_coefficient(images, texts, factor, own):
    logits = logit_scale * lax.dot_general(images, texts, CONTRACT, preferred_element_type=f32) + logit_bias
    matched = 0.0
    if own:
        i = lax.broadcasted_iota(jnp.int32, logits.shape, 0)
        j = lax.broadcasted_iota(jnp.int32, logits.shape, 1)
        hit = False
        for image_row, text_row, count in own:
            inside = (j >= text_row) & (j < text_row + count)
            hit = hit | (inside & (j - text_row == i - image_row))
        matched = hit.astype(f32)
    return (factor * (jax.nn.sigmoid(logits) - matched)).astype(bf16)


def pair_gradients(images, texts, coefficient):
    text_part = lax.dot_general(coefficient, images, LEADING, preferred_element_type=f32).astype(bf16)
    image_part = jnp.dot(coefficient, texts, preferred_element_type=f32)
    return text_part, image_part


def per_device(image_feat, image_weight, text_feat, text_weight):
    yl, core = lax.axis_index("yl"), lax.axis_index("core")
    rows_dev = image_feat.shape[0]
    share = rows_dev // 4
    batch_total = rows_dev * 32
    factor = loss_scale * logit_scale / batch_total

    text_got, text_rows = project(text_feat, text_weight, core)
    image_got, image_rows = project(image_feat, image_weight, core)
    text_sum = text_rows() + text_got
    text_sum, image_got = tie(text_sum, image_got)
    text_raw = sum_over_yl(text_sum, yl)
    image_raw = sum_over_yl(image_rows() + image_got, yl)
    text_unit, text_inverse = normalize(text_raw)
    image_unit, image_inverse = normalize(image_raw)

    text_halves = split(text_unit.astype(bf16), 2)
    one, two = direct_gather(text_halves[0], "x"), direct_gather(text_halves[1], "z")
    one, two, image_embed = tie(one, two, image_unit.astype(bf16))
    column = direct_gather(image_embed, "y")
    next_ = [shift(one, "z", 1), shift(one, "z", -1), shift(two, "x", 1), shift(two, "x", -1)]
    parts = [p for part in next_ for p in split(part, 2)]
    far = [shift(parts[0], "z", 1), shift(parts[3], "z", -1), shift(parts[4], "x", 1), shift(parts[7], "x", -1)]
    images = cat(column, shift(column, "core", 1))

    step = one.shape[0]
    next_texts, far_texts, near_texts = cat(*next_), far, cat(one, two)
    next_ = pair_gradients(images, next_texts, pair_coefficient(images, next_texts, factor, None))
    far_texts, next_ = tie(far_texts, next_)
    back = split(next_[0], 4)
    back = [shift(back[0], "z", -1), shift(back[1], "z", 1), shift(back[2], "x", -1), shift(back[3], "x", 1)]
    far_texts = cat(*far_texts)
    far = pair_gradients(images, far_texts, pair_coefficient(images, far_texts, factor, None))
    near_texts, far, back = tie(near_texts, far, back)
    own = [(0, 0, share // 2), (share // 2, step, share // 2)]
    coefficient = pair_coefficient(images, near_texts, factor, own)
    near = pair_gradients(images, near_texts, coefficient)
    image_grads = (near[1] + next_[1] + far[1]).astype(bf16)

    here, there = split(image_grads, 2)
    column = total(here, shift(there, "core", 1)).astype(bf16)
    near, far = split(near[0], 2), split(far[0], 2)
    one = total(near[0], back[0], back[1], shift(far[0], "z", 2)).astype(bf16)
    two = total(near[1], back[2], back[3], shift(far[1], "x", 2)).astype(bf16)
    image_embed_gradient = return_parts(split(column, 4), "y")
    one, two, image_embed_gradient = tie(one, two, image_embed_gradient)
    text_embed_gradient = cat(return_parts(split(one, 4), "x"), return_parts(split(two, 4), "z"))
    image_share = back_norm(image_embed_gradient, image_unit, image_inverse)
    image_raw_gradient = gather_over_mp(image_share, yl, core)
    image_terms = weight_terms(image_raw_gradient, image_feat)
    text_embed_gradient, image_terms = tie(text_embed_gradient, image_terms)
    image_weight_gradient = sum_over_loop(image_terms)
    text_share = back_norm(text_embed_gradient, text_unit, text_inverse)
    text_raw_gradient = gather_over_mp(text_share, yl, core)
    text_weight_gradient = sum_over_loop(weight_terms(text_raw_gradient, text_feat))
    image_feat_gradient = jnp.dot(image_raw_gradient, image_weight, preferred_element_type=f32).astype(bf16)
    text_feat_gradient = jnp.dot(text_raw_gradient, text_weight, preferred_element_type=f32).astype(bf16)
    return (image_feat_gradient, text_feat_gradient, image_weight_gradient, text_weight_gradient)


def solution(mesh):
    fine = Mesh(mesh.devices.reshape(tuple(SIZES.values())), tuple(SIZES))
    both = P(LOOP, MP)
    return jax.shard_map(
        per_device,
        mesh=fine,
        in_specs=(both, P(None, MP), both, P(None, MP)),
        out_specs=(both, both, both, both),
        check_vma=False,
    )
```

```python
import jax
import jax.numpy as jnp
from jax import lax
from jax.sharding import Mesh, PartitionSpec as P

logit_scale = 117.0
logit_bias = -12.7
loss_scale = 32768.0
epsilon = 1e-06

bf16 = jnp.bfloat16
f16 = jnp.float16
f32 = jnp.float32
SIZES = {"x": 4, "z": 4, "yh": 2, "yl": 2, "core": 2}
LOOP = ("x", "z", "yh")
MP = ("yl", "core")
CONTRACT = (((1,), (1,)), ((), ()))
LEADING = (((0,), (0,)), ((), ()))


def shift(value, axis, step):
    if axis == "y":
        return lax.ppermute(value, ("yh", "yl"), [(i, (i + step) % 4) for i in range(4)])
    n = SIZES[axis]
    return lax.ppermute(value, axis, [(i, (i + step) % n) for i in range(n)])


def cat(*parts):
    return jnp.concatenate(parts, axis=0)


def total(first, *rest):
    result = first.astype(f32)
    for part in rest:
        result = result + part.astype(f32)
    return result


def normalize(raw_rows):
    inverse = lax.rsqrt(jnp.sum(raw_rows * raw_rows, axis=1, keepdims=True) + epsilon)
    return (raw_rows * inverse, inverse)


def back_norm(gradient, unit_rows, inverse):
    inner = jnp.sum(unit_rows * gradient, axis=1, keepdims=True)
    return (inverse * (gradient - unit_rows * inner)).astype(bf16)


def half(value, index):
    rows = value.shape[0] // 2
    return lax.dynamic_slice_in_dim(value, index * rows, rows, axis=0)


def exchange_scaled(rows, axis):
    peak = jnp.max(jnp.abs(rows), axis=1, keepdims=True)
    exponent = jnp.clip(jnp.ceil(jnp.log2(peak)), -126.0, 126.0)
    scaled = (rows * jnp.exp2(-exponent)).astype(f16)
    column = jnp.broadcast_to(exponent.astype(f16), (rows.shape[0], 128))
    got = shift(jnp.concatenate((scaled, column), axis=1), axis, 1)
    width = rows.shape[1]
    return got[:, :width].astype(f32) * jnp.exp2(got[:, width : width + 1].astype(f32))


def project(feat, weight, yl, core):
    away = lax.dot_general(half(feat, 1 - core), weight, CONTRACT, preferred_element_type=f32)
    got = shift(away, "core", 1)
    rows = lax.dot_general(half(feat, core), weight, CONTRACT, preferred_element_type=f32) + got
    return half(rows, yl) + exchange_scaled(half(rows, 1 - yl), "yl")


def gather_over_mp(share, yl, core):
    got = shift(share, "yl", 1)
    first = yl == 0
    rows = cat(jnp.where(first, share, got), jnp.where(first, got, share))
    got = shift(rows, "core", 1)
    first = core == 0
    return cat(jnp.where(first, rows, got), jnp.where(first, got, rows))


STEPS = (1, -1, 2)


def direct_gather(block, axis):
    return cat(block, *[shift(block, axis, s) for s in STEPS])


def return_parts(parts, axis):
    return total(parts[0], *[shift(p, axis, -s) for p, s in zip(parts[1:], STEPS)])


def split(value, count):
    rows = value.shape[0] // count
    return [value[k * rows : (k + 1) * rows] for k in range(count)]


def tie(*values):
    return lax.optimization_barrier(values)


def block_terms(value, axis, index, dim):
    def block(step):
        return lax.dynamic_slice_in_dim(value, (index + step) % 4, 1, axis=dim)

    return [block(0)] + [shift(block(s), axis, s) for s in STEPS]


def pair_coefficient(images, texts, factor, own):
    logits = logit_scale * lax.dot_general(images, texts, CONTRACT, preferred_element_type=f32) + logit_bias
    matched = 0.0
    if own:
        i = lax.broadcasted_iota(jnp.int32, logits.shape, 0)
        j = lax.broadcasted_iota(jnp.int32, logits.shape, 1)
        hit = False
        for image_row, text_row, count in own:
            inside = (j >= text_row) & (j < text_row + count)
            hit = hit | (inside & (j - text_row == i - image_row))
        matched = hit.astype(f32)
    return (factor * (jax.nn.sigmoid(logits) - matched)).astype(bf16)


def pair_gradients(images, texts, coefficient):
    text_part = lax.dot_general(coefficient, images, LEADING, preferred_element_type=f32).astype(bf16)
    image_part = jnp.dot(coefficient, texts, preferred_element_type=f32)
    return text_part, image_part


def per_device(image_feat, image_weight, text_feat, text_weight):
    yl, core = lax.axis_index("yl"), lax.axis_index("core")
    rows_dev = image_feat.shape[0]
    share = rows_dev // 4
    batch_total = rows_dev * 32
    factor = loss_scale * logit_scale / batch_total

    text_raw = project(text_feat, text_weight, yl, core)
    image_raw = project(image_feat, image_weight, yl, core)
    text_unit, text_inverse = normalize(text_raw)
    image_unit, image_inverse = normalize(image_raw)

    text_halves = split(text_unit.astype(bf16), 2)
    one, two = direct_gather(text_halves[0], "x"), direct_gather(text_halves[1], "z")
    image_embed = image_unit.astype(bf16)
    one, two = tie(one, two)
    column = direct_gather(image_embed, "y")
    images = cat(column, shift(column, "core", 1))
    next_ = [shift(one, "z", 1), shift(one, "z", -1), shift(two, "x", 1), shift(two, "x", -1)]
    parts = [p for part in next_ for p in split(part, 2)]
    far = [shift(parts[0], "z", 1), shift(parts[3], "z", -1), shift(parts[4], "x", 1), shift(parts[7], "x", -1)]
    step = one.shape[0]
    own = [(0, 0, share // 2), (share // 2, step, share // 2)]
    next_texts, far_texts, near_texts = cat(*next_), cat(*far), cat(one, two)
    next_ = pair_gradients(images, next_texts, pair_coefficient(images, next_texts, factor, None))
    back = split(next_[0], 4)
    back = [shift(back[0], "z", -1), shift(back[1], "z", 1), shift(back[2], "x", -1), shift(back[3], "x", 1)]
    far = pair_gradients(images, far_texts, pair_coefficient(images, far_texts, factor, None))
    near = pair_gradients(images, near_texts, pair_coefficient(images, near_texts, factor, own))
    image_grads = (near[1] + next_[1] + far[1]).astype(bf16)

    here, there = split(image_grads, 2)
    column = total(here, shift(there, "core", 1)).astype(bf16)
    near, far = split(near[0], 2), split(far[0], 2)
    one = total(near[0], back[0], back[1], shift(far[0], "z", 2)).astype(bf16)
    two = total(near[1], back[2], back[3], shift(far[1], "x", 2)).astype(bf16)
    image_embed_gradient = return_parts(split(column, 4), "y")
    text_embed_gradient = cat(return_parts(split(one, 4), "x"), return_parts(split(two, 4), "z"))
    text_embed_gradient, image_embed_gradient = tie(text_embed_gradient, image_embed_gradient)
    image_share = back_norm(image_embed_gradient, image_unit, image_inverse)
    image_raw_gradient = gather_over_mp(image_share, yl, core)
    text_share = back_norm(text_embed_gradient, text_unit, text_inverse)
    text_raw_gradient = gather_over_mp(text_share, yl, core)

    depth = image_weight.shape[0]
    x, z, yh = lax.axis_index("x"), lax.axis_index("z"), lax.axis_index("yh")
    columns = image_feat.shape[1]
    cut = 1024

    def weight_part(raw_gradient, feat):
        part = lax.dot_general(raw_gradient, feat, LEADING, preferred_element_type=f32).astype(bf16)
        return part.reshape(4, 4, depth // 16, feat.shape[1])

    one = weight_part(image_raw_gradient, image_feat[:, :cut])
    two = jnp.concatenate(
        (weight_part(image_raw_gradient, image_feat[:, cut:]), weight_part(text_raw_gradient, text_feat)), axis=3
    )
    one = block_terms(one, "x", x, 0)
    two = block_terms(two, "z", z, 1)
    one = total(*block_terms(total(*one).astype(bf16), "z", z, 1))
    two = total(*block_terms(total(*two).astype(bf16), "x", x, 0))
    rows = jnp.concatenate((one, two), axis=3).reshape(depth // 16, columns + text_feat.shape[1])
    got = shift(half(rows, 1 - yh).astype(bf16), "yh", 1)
    rows = half(rows, yh)
    image_weight_gradient = total(rows[:, :columns], got[:, :columns])
    text_weight_gradient = total(rows[:, columns:], got[:, columns:])
    image_feat_gradient = jnp.dot(image_raw_gradient, image_weight, preferred_element_type=f32).astype(bf16)
    text_feat_gradient = jnp.dot(text_raw_gradient, text_weight, preferred_element_type=f32).astype(bf16)
    return (image_feat_gradient, text_feat_gradient, image_weight_gradient, text_weight_gradient)


def solution(mesh):
    fine = Mesh(mesh.devices.reshape(tuple(SIZES.values())), tuple(SIZES))
    both = P(LOOP, MP)
    return jax.shard_map(
        per_device,
        mesh=fine,
        in_specs=(both, P(None, MP), both, P(None, MP)),
        out_specs=(both, both, both, both),
        check_vma=False,
    )
```

```python
import jax
import jax.numpy as jnp
from jax import lax
from jax.sharding import Mesh, PartitionSpec as P

logit_scale = 117.0
logit_bias = -12.7
loss_scale = 32768.0
epsilon = 1e-06

bf16 = jnp.bfloat16
f16 = jnp.float16
f32 = jnp.float32
SIZES = {"x": 4, "z": 4, "yh": 2, "yl": 2, "core": 2}
LOOP = ("x", "z", "yh")
MP = ("yl", "core")
CONTRACT = (((1,), (1,)), ((), ()))
LEADING = (((0,), (0,)), ((), ()))


def shift(value, axis, step):
    if axis == "y":
        return lax.ppermute(value, ("yh", "yl"), [(i, (i + step) % 4) for i in range(4)])
    n = SIZES[axis]
    return lax.ppermute(value, axis, [(i, (i + step) % n) for i in range(n)])


def cat(*parts):
    return jnp.concatenate(parts, axis=0)


def total(first, *rest):
    result = first.astype(f32)
    for part in rest:
        result = result + part.astype(f32)
    return result


def normalize(raw_rows):
    inverse = lax.rsqrt(jnp.sum(raw_rows * raw_rows, axis=1, keepdims=True) + epsilon)
    return (raw_rows * inverse, inverse)


def back_norm(gradient, unit_rows, inverse):
    inner = jnp.sum(unit_rows * gradient, axis=1, keepdims=True)
    return (inverse * (gradient - unit_rows * inner)).astype(bf16)


def half(value, index):
    rows = value.shape[0] // 2
    return lax.dynamic_slice_in_dim(value, index * rows, rows, axis=0)


def exchange_scaled(rows, axis):
    peak = jnp.max(jnp.abs(rows), axis=1, keepdims=True)
    exponent = jnp.clip(jnp.ceil(jnp.log2(peak)), -126.0, 126.0)
    scaled = (rows * jnp.exp2(-exponent)).astype(f16)
    column = jnp.broadcast_to(exponent.astype(f16), (rows.shape[0], 128))
    got = shift(jnp.concatenate((scaled, column), axis=1), axis, 1)
    width = rows.shape[1]
    return got[:, :width].astype(f32) * jnp.exp2(got[:, width : width + 1].astype(f32))


def project(feat, weight, yl, core):
    away = lax.dot_general(half(feat, 1 - core), weight, CONTRACT, preferred_element_type=f32)
    got = shift(away, "core", 1)
    rows = lax.dot_general(half(feat, core), weight, CONTRACT, preferred_element_type=f32) + got
    return half(rows, yl) + exchange_scaled(half(rows, 1 - yl), "yl")


def gather_over_mp(share, yl, core):
    got = shift(share, "yl", 1)
    first = yl == 0
    rows = cat(jnp.where(first, share, got), jnp.where(first, got, share))
    got = shift(rows, "core", 1)
    first = core == 0
    return cat(jnp.where(first, rows, got), jnp.where(first, got, rows))


STEPS = (1, -1, 2)


def direct_gather(block, axis):
    return cat(block, *[shift(block, axis, s) for s in STEPS])


def return_parts(parts, axis):
    return total(parts[0], *[shift(p, axis, -s) for p, s in zip(parts[1:], STEPS)])


def split(value, count):
    rows = value.shape[0] // count
    return [value[k * rows : (k + 1) * rows] for k in range(count)]


def ring_terms(value, axis, index, dim):
    def block(step):
        return lax.dynamic_slice_in_dim(value, (index + step) % 4, 1, axis=dim)

    left, right = jnp.split(block(2), 2, axis=3)
    up, down = jnp.split(block(1), 2, axis=3), jnp.split(block(-1), 2, axis=3)
    up[0] = total(up[0], shift(left, axis, 1)).astype(bf16)
    down[1] = total(down[1], shift(right, axis, -1)).astype(bf16)
    return [block(0), shift(jnp.concatenate(up, axis=3), axis, 1), shift(jnp.concatenate(down, axis=3), axis, -1)]


def tie(*values):
    return lax.optimization_barrier(values)


def block_terms(value, axis, index, dim):
    def block(step):
        return lax.dynamic_slice_in_dim(value, (index + step) % 4, 1, axis=dim)

    return [block(0)] + [shift(block(s), axis, s) for s in STEPS]


def pair_coefficient(images, texts, factor, own):
    logits = logit_scale * lax.dot_general(images, texts, CONTRACT, preferred_element_type=f32) + logit_bias
    matched = 0.0
    if own:
        i = lax.broadcasted_iota(jnp.int32, logits.shape, 0)
        j = lax.broadcasted_iota(jnp.int32, logits.shape, 1)
        hit = False
        for image_row, text_row, count in own:
            inside = (j >= text_row) & (j < text_row + count)
            hit = hit | (inside & (j - text_row == i - image_row))
        matched = hit.astype(f32)
    return (factor * (jax.nn.sigmoid(logits) - matched)).astype(bf16)


def pair_gradients(images, texts, coefficient):
    text_part = lax.dot_general(coefficient, images, LEADING, preferred_element_type=f32).astype(bf16)
    image_part = jnp.dot(coefficient, texts, preferred_element_type=f32)
    return text_part, image_part


def per_device(image_feat, image_weight, text_feat, text_weight):
    yl, core = lax.axis_index("yl"), lax.axis_index("core")
    rows_dev = image_feat.shape[0]
    share = rows_dev // 4
    batch_total = rows_dev * 32
    factor = loss_scale * logit_scale / batch_total

    text_raw = project(text_feat, text_weight, yl, core)
    image_raw = project(image_feat, image_weight, yl, core)
    text_unit, text_inverse = normalize(text_raw)
    image_unit, image_inverse = normalize(image_raw)

    text_halves = split(text_unit.astype(bf16), 2)
    one, two = direct_gather(text_halves[0], "x"), direct_gather(text_halves[1], "z")
    image_embed = image_unit.astype(bf16)
    one, two = tie(one, two)
    column = direct_gather(image_embed, "y")
    images = cat(column, shift(column, "core", 1))
    next_ = [shift(one, "z", 1), shift(one, "z", -1), shift(two, "x", 1), shift(two, "x", -1)]
    parts = [p for part in next_ for p in split(part, 2)]
    far = [shift(parts[0], "z", 1), shift(parts[3], "z", -1), shift(parts[4], "x", 1), shift(parts[7], "x", -1)]
    step = one.shape[0]
    own = [(0, 0, share // 2), (share // 2, step, share // 2)]
    next_texts, far_texts, near_texts = cat(*next_), cat(*far), cat(one, two)
    next_ = pair_gradients(images, next_texts, pair_coefficient(images, next_texts, factor, None))
    back = split(next_[0], 4)
    back = [shift(back[0], "z", -1), shift(back[1], "z", 1), shift(back[2], "x", -1), shift(back[3], "x", 1)]
    far = pair_gradients(images, far_texts, pair_coefficient(images, far_texts, factor, None))
    near = pair_gradients(images, near_texts, pair_coefficient(images, near_texts, factor, own))
    image_grads = (near[1] + next_[1] + far[1]).astype(bf16)

    here, there = split(image_grads, 2)
    column = total(here, shift(there, "core", 1)).astype(bf16)
    near, far = split(near[0], 2), split(far[0], 2)
    one = total(near[0], back[0], back[1], shift(far[0], "z", 2)).astype(bf16)
    two = total(near[1], back[2], back[3], shift(far[1], "x", 2)).astype(bf16)
    image_embed_gradient = return_parts(split(column, 4), "y")
    text_embed_gradient = cat(return_parts(split(one, 4), "x"), return_parts(split(two, 4), "z"))
    text_embed_gradient, image_embed_gradient = tie(text_embed_gradient, image_embed_gradient)
    image_share = back_norm(image_embed_gradient, image_unit, image_inverse)
    image_raw_gradient = gather_over_mp(image_share, yl, core)
    text_share = back_norm(text_embed_gradient, text_unit, text_inverse)
    text_raw_gradient = gather_over_mp(text_share, yl, core)

    depth = image_weight.shape[0]
    x, z, yh = lax.axis_index("x"), lax.axis_index("z"), lax.axis_index("yh")
    columns = image_feat.shape[1]
    cut = 1024

    def weight_part(raw_gradient, feat):
        part = lax.dot_general(raw_gradient, feat, LEADING, preferred_element_type=f32).astype(bf16)
        return part.reshape(4, 4, depth // 16, feat.shape[1])

    one = weight_part(image_raw_gradient, image_feat[:, :cut])
    two = jnp.concatenate(
        (weight_part(image_raw_gradient, image_feat[:, cut:]), weight_part(text_raw_gradient, text_feat)), axis=3
    )
    one = ring_terms(one, "x", x, 0)
    two = ring_terms(two, "z", z, 1)
    one = total(*block_terms(total(*one).astype(bf16), "z", z, 1))
    two = total(*block_terms(total(*two).astype(bf16), "x", x, 0))
    rows = jnp.concatenate((one, two), axis=3).reshape(depth // 16, columns + text_feat.shape[1])
    got = shift(half(rows, 1 - yh).astype(bf16), "yh", 1)
    rows = half(rows, yh)
    image_weight_gradient = total(rows[:, :columns], got[:, :columns])
    text_weight_gradient = total(rows[:, columns:], got[:, columns:])
    image_feat_gradient = jnp.dot(image_raw_gradient, image_weight, preferred_element_type=f32).astype(bf16)
    text_feat_gradient = jnp.dot(text_raw_gradient, text_weight, preferred_element_type=f32).astype(bf16)
    return (image_feat_gradient, text_feat_gradient, image_weight_gradient, text_weight_gradient)


def solution(mesh):
    fine = Mesh(mesh.devices.reshape(tuple(SIZES.values())), tuple(SIZES))
    both = P(LOOP, MP)
    return jax.shard_map(
        per_device,
        mesh=fine,
        in_specs=(both, P(None, MP), both, P(None, MP)),
        out_specs=(both, both, both, both),
        check_vma=False,
    )
```
